256 devices in a mesh: dp: 4 (over x), expert: 64 (over y, z, core).
Axes of the slice: x: 4, y: 4, z: 8, core: 2. Of those that a mesh axis runs over, the one named last changes fastest.
Arguments:
- grad_out: bfloat16 [32768, 3584], P(('dp', 'expert')), may hold values from -6 to 6
- expert_ids: int32 [32768, 8], P(('dp', 'expert')), may hold values from 0 to 63, all different within a row; in each aligned block of 128 rows (0 to 127, 128 to 255, ...) at most 24 rows name the same one
- gate_weights: float32 [32768, 8], P(('dp', 'expert')), may hold values from 0.05 to 0.4
- hidden_saved: bfloat16 [4, 64, 64, 24, 1024], P('dp', 'expert'), may hold values from -6 to 6
- swap_flags: int32 [64], replicated, may hold values from 0 to 1, as said below
Outputs:
- panel_grads: float32 [64, 3584, 1024], P('expert', 'dp')
The draws below stay inside these ranges and needn't reach their ends.
Inputs may be any that keep to these rules, and one draw needn't show every extreme that they name: `expert_ids`: each row names 8 different experts; the rows of one device name no expert more than 24 times, and in some devices one expert exactly 24 times. swap_flags[e] = swap_flags[(e + 32) mod 64]; swap_flags[0] = swap_flags[31] = 1 and swap_flags[1] = 0.
All inputs are finite; a program needn't handle non-finite values.
Results may differ from the reference program's by a relative error of at most 0.0029.
Values may be sent and summed in bfloat16 or wider, within the bound.
No kernel may reach another device: no remote copies, remote signals or barrier semaphores. Data moves between devices by JAX's collectives and lax.ppermute only.
A program may use at most 128 MiB of HBM per device.

```python
import math
import jax
import jax.numpy as jnp
import numpy as np
from jax import lax

D = 3584
H = 1024
TOP = 8
TOK_DEV = 128
EXPERTS = 64
CAP = 24
TOKENS = 32768
N_DP = 4
N_EXPERT = 64


def draw_swap_flags(key, part):
    key = jax.random.fold_in(key, 11)
    halfway = EXPERTS // 2
    paired = jax.random.randint(key, (halfway,), 0, 2)
    paired = paired.at[0].set(1)
    paired = paired.at[halfway - 1].set(1)
    paired = paired.at[1].set(0)
    return jnp.concatenate([paired, paired]).astype(jnp.int32)


def block_scale(stream_key, dims, shards, smallest, top_value):
    gain = 1.0
    for dim, parts in shards:
        steps = jax.random.uniform(jax.random.fold_in(jax.random.fold_in(stream_key, 6), dim), (parts,), jnp.float32, smallest / len(shards), top_value / len(shards))
        gain = gain * jnp.repeat(jnp.exp(steps), dims[dim] // parts).reshape((-1,) + (1,) * (len(dims) - 1 - dim))
    return gain


def deal_out(own_key, own, number, rows, amount, top, bound, lean):
    sequence = jax.random.permutation(own_key, amount)
    packed, common = shares(amount, rows * top, bound, lean, True), shares(amount, rows * top, bound, lean, False)
    places = jnp.arange(amount)

    def named(sizes, offset_by):
        used = int((sizes > 0).sum())
        fixed = max(1, used // 4)
        shifted = fixed + (places - fixed + offset_by * (used - fixed)) % max(1, amount - fixed)
        return jnp.zeros((amount,), jnp.int32).at[sequence[jnp.where(places < fixed, places, shifted)]].set(jnp.asarray(sizes, jnp.int32))

    sizes = jnp.where(number % 4 == 0, named(packed, number // 4), named(common, number - number // 4 - 1))
    mixed = jax.random.permutation(jax.random.fold_in(own, 3), amount)
    giver, receiver = mixed[0:amount // 2 * 2:2], mixed[1:amount // 2 * 2:2]
    room = jnp.minimum(sizes[giver] - 1, bound - sizes[receiver]) // 2
    room = jnp.where((giver == sequence[0]) | (receiver == sequence[0]) | (sizes[receiver] == 0), 0, jnp.maximum(room, 0))
    shifted = jax.random.randint(jax.random.fold_in(own, 4), (amount // 2,), 0, 1 << 20) % (room + 1)
    sizes = sizes.at[giver].add(-shifted).at[receiver].add(shifted)
    members = jnp.searchsorted(jnp.cumsum(sizes), jnp.arange(rows * top), side="right").astype(jnp.int32)
    listing = members.reshape(top, rows).T
    listing = listing[jax.random.permutation(jax.random.fold_in(own, 1), rows)]
    offset_by = jax.random.randint(jax.random.fold_in(own, 2), (rows, 1), 0, top)
    return jnp.take_along_axis(listing, (jnp.arange(top)[None, :] + offset_by) % top, axis=1)


def shares(amount, total, limit, lean, full):
    loads = [(1 << 20) // math.isqrt(standing ** lean) + 1 for standing in range(1, amount + 1)]
    largest = limit if full else min(limit, max(-(-total // amount), total * loads[0] // sum(loads)))
    least = 1 if total - largest >= amount - 1 else 0
    counts, spare = [largest] + [least] * (amount - 1), total - largest - least * (amount - 1)
    while spare > 0:
        candidates = [i for i in range(1, amount) if counts[i] < largest] or [i for i in range(1, amount) if counts[i] < limit]
        mass, remaining = sum([loads[i] for i in candidates]), spare
        for i in candidates:
            more = min(limit - counts[i], max(1, remaining * loads[i] // mass), spare)
            counts[i] = counts[i] + more
            spare = spare - more
    return np.array(counts)


def gaussian(rng, shape, width, bound, shards=(), kind=jnp.bfloat16):
    array = jax.random.normal(rng, shape, jnp.float32) * width
    if len(shards) > 0:
        array = block_scale(rng, shape, shards, -0.22, 0.18) * array
    return jnp.clip(array, min=-bound, max=bound).astype(kind)


def setup_inputs(seed: int = 0) -> dict:
    splits = jax.random.split(jax.random.key(seed), 6)
    grad_out = gaussian(splits[0], (TOKENS, D), 1.0, 6.0, ((0, 256),))
    expert_ids_keys = jax.random.split(jax.random.fold_in(splits[1], 1), TOKENS // TOK_DEV)
    expert_ids_turns = jax.random.permutation(jax.random.fold_in(splits[1], 3), TOKENS // TOK_DEV)
    expert_ids = jax.vmap(lambda own, number: deal_out(jax.random.fold_in(splits[1], 2), own, number, TOK_DEV, EXPERTS, TOP, CAP, 2))(expert_ids_keys, expert_ids_turns).reshape((TOKENS, TOP))
    gate_weights = jnp.clip(0.05 + 0.35 * jax.random.uniform(splits[2], (TOKENS, TOP), jnp.float32) ** block_scale(splits[2], (TOKENS, TOP), ((0, 256),), -0.2, 0.2), 0.05, 0.4)
    hidden_saved = gaussian(splits[3], (N_DP, EXPERTS, N_EXPERT, CAP, H), 1.0, 6.0, ((0, 4), (1, 64)))
    swap_flags = draw_swap_flags(jax.random.fold_in(splits[5], 71), 0)
    return {"grad_out": grad_out, "expert_ids": expert_ids, "gate_weights": gate_weights, "hidden_saved": hidden_saved, "swap_flags": swap_flags}


def slot_positions(routed):
    onehot = (routed[..., None] == jnp.arange(EXPERTS, dtype=jnp.int32)).astype(jnp.int32)
    return lax.optimization_barrier(jnp.sum(onehot * (jnp.cumsum(onehot, axis=-2) - 1), axis=-1)).astype(jnp.int32)

def reference(grad_out, expert_ids, gate_weights, hidden_saved, swap_flags):
    sources = N_DP * N_EXPERT
    fanout = TOK_DEV * TOP
    routed = expert_ids.reshape(sources, fanout)
    position = slot_positions(routed)
    target = (routed * CAP + position).astype(jnp.int32)
    inverse = jnp.full((sources, EXPERTS * CAP), fanout, jnp.int32)
    source_range = jnp.arange(sources, dtype=jnp.int32)[:, None]
    order = jnp.broadcast_to(jnp.arange(fanout, dtype=jnp.int32)[None], (sources, fanout))
    inverse = inverse.at[source_range, target].set(order).reshape(sources, EXPERTS, CAP)
    grad_rows = grad_out.reshape(sources, TOK_DEV, D)
    gates = gate_weights.reshape(sources, fanout)

    def expert_grad(expert):
        picked = lax.dynamic_index_in_dim(inverse, expert, 1, False)
        in_use = picked < fanout
        clipped = jnp.minimum(picked, fanout - 1).astype(jnp.int32)
        token_index = (clipped // TOP).astype(jnp.int32)
        row_block = jnp.take_along_axis(grad_rows, token_index[:, :, None], axis=1)
        weight = jnp.take_along_axis(gates, clipped, axis=1)
        weight = jnp.where(in_use, weight, jnp.zeros_like(weight))
        scaled = (weight[:, :, None] * row_block.astype(jnp.float32)).astype(jnp.bfloat16)
        scaled = scaled.reshape(sources * CAP, D)
        states = lax.dynamic_index_in_dim(hidden_saved, expert, 1, False).reshape(sources * CAP, H)
        return jnp.dot(scaled.T, states, preferred_element_type=jnp.float32)
    expert_grads = lax.map(expert_grad, jnp.arange(EXPERTS, dtype=jnp.int32))
    halfway = EXPERTS // 2
    expert_range = jnp.arange(EXPERTS, dtype=jnp.int32)
    host_index = jnp.where(swap_flags == 1, (expert_range + halfway) % EXPERTS, expert_range).astype(jnp.int32)
    return jnp.take(expert_grads, host_index, axis=0)
```

```python
import jax
import jax.numpy as jnp
from jax import lax
from jax.experimental import pallas as pl
from jax.experimental.pallas import tpu as pltpu
from jax.sharding import Mesh, PartitionSpec as P

NX, NY, NZ, NC = 4, 4, 8, 2
OFFSETS = [(dy, dc) for dy in range(NY) for dc in range(NC)]


def dispatch_kernel(target_ref, gate_ref, token_ref, *out_refs):
    rows = out_refs[0].shape[0]
    tokens = target_ref.shape[2]
    slot = lax.broadcasted_iota(jnp.int32, (rows, tokens), 0).astype(jnp.float32)
    picks, weights = [], []
    for r in range(len(out_refs)):
        hit = slot == target_ref[0, r : r + 1, :]
        picks.append(jnp.where(hit, 1.0, 0.0))
        weights.append(jnp.sum(jnp.where(hit, gate_ref[0, r : r + 1, :], 0.0), axis=1, keepdims=True))
    pick = jnp.concatenate(picks, axis=0).astype(jnp.bfloat16)
    weight = jnp.concatenate(weights, axis=0)
    block = token_ref[...].reshape(tokens, token_ref.shape[-1])
    scaled = jnp.dot(pick, block, preferred_element_type=jnp.float32) * weight
    scaled = scaled.astype(jnp.bfloat16)
    for r, out in enumerate(out_refs):
        out[...] = scaled[r * rows : (r + 1) * rows]


def dispatch(target, gate, tokens, capacity):
    pairs, dests, width = target.shape
    rows, cols = 2 * capacity, tokens.shape[-1]
    return pl.pallas_call(
        dispatch_kernel,
        grid=(pairs,),
        in_specs=[
            pl.BlockSpec((1, dests, width), lambda i: (i, 0, 0)),
            pl.BlockSpec((1, dests, width), lambda i: (i, 0, 0)),
            pl.BlockSpec((2, width // 2, cols), lambda i: (i, 0, 0)),
        ],
        out_specs=[pl.BlockSpec((rows, cols), lambda i: (i, 0))] * dests,
        out_shape=[jax.ShapeDtypeStruct((pairs * rows, cols), jnp.bfloat16)] * dests,
        compiler_params=pltpu.CompilerParams(vmem_limit_bytes=40 * 1024 * 1024),
        cost_estimate=pl.CostEstimate(
            flops=2 * pairs * dests * rows * width * cols,
            bytes_accessed=pairs * (width + dests * rows) * cols * 2,
            transcendentals=0,
        ),
    )(target, gate, tokens)


def ring(axis_size, step):
    return [(i, (i + step) % axis_size) for i in range(axis_size)]


def plane_pairs(dy, dc):
    return [(y * NC + c, ((y + dy) % NY) * NC + (c ^ dc)) for y in range(NY) for c in range(NC)]


def local(grad_out, expert_ids, gate_weights, hidden_saved, swap_flags):
    x, y = lax.axis_index("x"), lax.axis_index("y")
    z, c = lax.axis_index("z"), lax.axis_index("c")
    experts, capacity, hidden_cols = hidden_saved.shape[2:]
    tok, cols = grad_out.shape[0], grad_out.shape[1] // NX
    top = expert_ids.shape[1]

    flag_here = lax.dynamic_index_in_dim(swap_flags, (y * NZ + z) * NC + c, 0, False)
    hidden = hidden_saved.reshape(NY, NZ, NC, capacity, hidden_cols)
    traded = lax.ppermute(hidden, "y", ring(NY, 2))

    def columns(step):
        return lax.dynamic_slice_in_dim(grad_out, ((x + step) % NX) * cols, cols, 1)

    steps = (0, 1, 3, 2)
    mine = jnp.stack([columns(0)] + [lax.ppermute(columns(s), "x", ring(NX, s)) for s in steps[1:]])
    gathered = lax.all_gather(mine, "z", axis=1)

    meta = jnp.concatenate([expert_ids.astype(jnp.float32).T, gate_weights.T], axis=0)
    meta = jnp.broadcast_to(meta[None], (NX * NZ,) + meta.shape)
    meta = lax.all_to_all(meta, ("x", "z"), 0, 0, tiled=True)
    ids, gates = meta[:, :top], meta[:, top:]
    devices = jnp.stack([(((y + dy) % NY) * NZ + z) * NC + (c ^ dc) for dy, dc in OFFSETS])
    flags = jnp.take(swap_flags, devices)
    wanted = jnp.where(flags == 1, (devices + experts // 2) % experts, devices).astype(jnp.float32)
    match = ids[:, None] == wanted[None, :, None, None]
    member = jnp.any(match, axis=2)
    gate = jnp.sum(jnp.where(match, gates[:, None], 0.0), axis=2)
    before = (jnp.arange(tok)[:, None] < jnp.arange(tok)[None, :]).astype(jnp.bfloat16)
    slot = jnp.dot(member.astype(jnp.bfloat16), before, preferred_element_type=jnp.float32)
    odd = (jnp.arange(NX * NZ) % 2 * capacity).astype(jnp.float32)
    target = jnp.where(member, slot + odd[:, None, None], -1.0)

    def paired(table):
        table = table.reshape(NX, NZ // 2, 2, len(OFFSETS), tok).transpose(0, 1, 3, 2, 4)
        return table.reshape(NX, NZ // 2, len(OFFSETS), 2 * tok)

    target, gate = paired(target), paired(gate)

    hidden = jnp.where(flag_here == 1, traded, hidden).transpose(0, 2, 1, 3, 4)
    hidden = hidden.reshape(NY * NC, NZ * capacity, hidden_cols)
    order = [((y - dy) % NY) * NC + (c ^ dc) for dy, dc in OFFSETS]
    hidden = jnp.concatenate([lax.dynamic_index_in_dim(hidden, o, 0, False) for o in order], axis=0)
    states = [hidden] + [lax.ppermute(hidden, "x", ring(NX, s)) for s in steps[1:]]

    total = None
    for i, s in enumerate(steps):
        source = (x - s) % NX
        rows = dispatch(
            lax.dynamic_index_in_dim(target, source, 0, False),
            lax.dynamic_index_in_dim(gate, source, 0, False),
            gathered[i],
            capacity,
        )
        pieces = [rows[0]] + [
            lax.ppermute(rows[r], ("y", "c"), plane_pairs(*OFFSETS[r])) for r in range(1, len(OFFSETS))
        ]
        received = jnp.concatenate(pieces, axis=0)
        term = lax.dot_general(
            received, states[i], (((0,), (0,)), ((), ())), preferred_element_type=jnp.float32
        )
        total = term if total is None else total + term
    return total[None]


def solution(mesh):
    fine = Mesh(mesh.devices.reshape(NX, NY, NZ, NC), ("x", "y", "z", "c"))
    every = ("x", "y", "z", "c")
    return jax.shard_map(
        local,
        mesh=fine,
        in_specs=(
            P(every, None),
            P(every, None),
            P(every, None),
            P("x", ("y", "z", "c"), None, None, None),
            P(),
        ),
        out_specs=P(("y", "z", "c"), "x", None),
        check_vma=False,
    )
```

```python
import functools

import jax
import jax.numpy as jnp
from jax import lax
from jax.experimental import pallas as pl
from jax.experimental.pallas import tpu as pltpu
from jax.sharding import Mesh, PartitionSpec as P

NX, NY, NZ, NC = 4, 4, 8, 2
GATHERS = ((0, 1), (3, 2))
SPACE = 56 * 1024 * 1024
PARTS = 3
META = 128
LIGHT = pl.CostEstimate(flops=1024, bytes_accessed=1024, transcendentals=0)


def dispatch_kernel(target_ref, gate_ref, token_ref, *refs):
    out_ref = refs[-1]
    dests, rows = out_ref.shape[:2]
    tokens = target_ref.shape[2]
    slot = lax.broadcasted_iota(jnp.int32, (rows, tokens), 0).astype(jnp.float32)
    picks, weights = [], []
    for r in range(dests):
        hit = slot == target_ref[0, r : r + 1, :]
        picks.append(jnp.where(hit, 1.0, 0.0))
        weights.append(jnp.sum(jnp.where(hit, gate_ref[0, r : r + 1, :], 0.0), axis=1, keepdims=True))
    pick = jnp.concatenate(picks, axis=0).astype(jnp.bfloat16)
    weight = jnp.concatenate(weights, axis=0)
    scaled = jnp.dot(pick, token_ref[...], preferred_element_type=jnp.float32) * weight
    scaled = scaled.astype(jnp.bfloat16)
    for r in range(dests):
        out_ref[r] = scaled[r * rows : (r + 1) * rows]


def dispatch(target, gate, tokens, cols, capacity, after=()):
    pairs, dests, width = target.shape
    rows = 2 * capacity
    return pl.pallas_call(
        dispatch_kernel,
        grid=(pairs,),
        in_specs=[
            pl.BlockSpec((1, dests, width), lambda i: (i, 0, 0)),
            pl.BlockSpec((1, dests, width), lambda i: (i, 0, 0)),
            pl.BlockSpec((width, cols), lambda i: (i, 0)),
        ]
        + [pl.BlockSpec(memory_space=pl.ANY)] * len(after),
        out_specs=pl.BlockSpec((dests, rows, cols), lambda i: (0, i, 0)),
        out_shape=jax.ShapeDtypeStruct((dests, pairs * rows, cols), jnp.bfloat16),
        compiler_params=pltpu.CompilerParams(vmem_limit_bytes=SPACE),
        cost_estimate=LIGHT,
    )(target, gate, tokens, *after)


def later_kernel(value_ref, *refs):
    refs[-1][0] = value_ref[0]


def later(value, *after):
    return pl.pallas_call(
        later_kernel,
        in_specs=[pl.BlockSpec(memory_space=pltpu.SMEM)] + [pl.BlockSpec(memory_space=pl.ANY)] * len(after),
        out_specs=pl.BlockSpec(memory_space=pltpu.SMEM),
        out_shape=jax.ShapeDtypeStruct((1,), jnp.int32),
        cost_estimate=LIGHT,
    )(jnp.asarray(value, jnp.int32).reshape(1), *after)[0]


def ring(size, step):
    return [(i, (i + step) % size) for i in range(size)]


def routing(ids, gates):
    columns = [ids.astype(jnp.float32)]
    for _ in range(PARTS):
        high = lax.reduce_precision(gates, 8, 7)
        columns.append(high)
        gates = gates - high
    meta = jnp.concatenate(columns, axis=1)
    return jnp.pad(meta, ((0, 0), (0, META - meta.shape[1]))).astype(jnp.bfloat16)


def tables(meta, tok, top, wanted, capacity):
    sources = meta.shape[0] // tok
    meta = meta.astype(jnp.float32).reshape(sources, tok, -1).transpose(0, 2, 1)
    ids, gates = meta[:, :top], 0.0
    for i in reversed(range(PARTS)):
        gates = gates + meta[:, (i + 1) * top : (i + 2) * top]
    match = ids[:, None] == wanted[None, :, None, None]
    member = jnp.any(match, axis=2)
    gate = jnp.sum(jnp.where(match, gates[:, None], 0.0), axis=2)
    before = (jnp.arange(tok)[:, None] < jnp.arange(tok)[None, :]).astype(jnp.bfloat16)
    slot = jnp.dot(member.astype(jnp.bfloat16), before, preferred_element_type=jnp.float32)
    odd = (jnp.arange(sources) % 2 * capacity).astype(jnp.float32)
    target = jnp.where(member, slot + odd[:, None, None], -1.0)

    def paired(table):
        table = table.reshape(sources // 2, 2, len(wanted), tok).transpose(0, 2, 1, 3)
        return table.reshape(sources // 2, len(wanted), 2 * tok)

    return paired(target), paired(gate)


def product_kernel(spans, *refs):
    rows_ref, states, out_ref = refs[0], refs[1 : 1 + len(spans)], refs[-1]
    step = pl.program_id(0)

    @pl.when(step == 0)
    def _():
        out_ref[...] = refs[-2][...] if len(refs) > len(spans) + 2 else jnp.zeros_like(out_ref)

    depth, width = states[0].shape[1:]

    def add(chunk, states_ref):
        rows = rows_ref[:, chunk * depth : (chunk + 1) * depth, :]
        out_ref[...] += lax.dot_general(
            rows.reshape(-1, rows.shape[-1]),
            states_ref[...].reshape(-1, width),
            (((0,), (0,)), ((), ())),
            preferred_element_type=jnp.float32,
        )

    for (chunk, low, high), states_ref in zip(spans, states):
        pl.when((step >= low) & (step < high))(functools.partial(add, chunk, states_ref))


def product(total, rows, states):
    senders, _, cols = rows.shape
    group = senders // 2
    depth, width = states[0][0].shape[1:]
    whole = pl.BlockSpec((cols, width), lambda i: (0, 0))
    spans, arrays, specs = [], [], []
    for chunk, parts in enumerate(states):
        low = 0
        for array in parts:
            count = array.shape[0] // group
            spans.append((chunk, low, low + count))
            arrays.append(array)
            specs.append(
                pl.BlockSpec(
                    (group, depth, width),
                    functools.partial(lambda low, count, i: (jnp.clip(i - low, 0, count - 1), 0, 0), low, count),
                )
            )
            low += count
    return pl.pallas_call(
        functools.partial(product_kernel, tuple(spans)),
        grid=(senders // group,),
        in_specs=[pl.BlockSpec((group,) + rows.shape[1:], lambda i: (i, 0, 0))]
        + specs
        + ([] if total is None else [whole]),
        out_specs=whole,
        out_shape=jax.ShapeDtypeStruct((cols, width), jnp.float32),
        compiler_params=pltpu.CompilerParams(vmem_limit_bytes=SPACE),
        cost_estimate=LIGHT,
    )(rows, *arrays, *([] if total is None else [total]))


def local(grad_out, expert_ids, gate_weights, hidden_saved, swap_flags):
    x, y = lax.axis_index("x"), lax.axis_index("y")
    z, c = lax.axis_index("z"), lax.axis_index("c")
    experts, capacity, width = hidden_saved.shape[2:]
    tok, cols = grad_out.shape[0], grad_out.shape[1] // NX
    top = expert_ids.shape[1]
    flag_here = lax.dynamic_index_in_dim(swap_flags, (y * NZ + z) * NC + c, 0, False)
    hidden = hidden_saved.reshape(NY, NZ, NC, capacity, width)
    traded = lax.ppermute(hidden, "y", ring(NY, 2))

    meta = routing(expert_ids, gate_weights)

    def columns(step):
        part = lax.dynamic_slice_in_dim(grad_out, ((x + step) % NX) * cols, cols, 1)
        part = jnp.concatenate([part, meta], axis=1)
        return part if step == 0 else lax.ppermute(part, "x", ring(NX, step))

    gathered = []
    for group in GATHERS:
        block = jnp.stack([columns(s) for s in group])
        gathered.append(lax.all_gather(block, "z", axis=1, tiled=True).reshape(-1, cols + META))

    devices = ((jnp.arange(NY)[:, None] * NZ + z) * NC + jnp.arange(NC)[None]).reshape(-1)
    flags = jnp.take(swap_flags, devices)
    wanted = jnp.where(flags == 1, (devices + experts // 2) % experts, devices).astype(jnp.float32)

    def exchange(tokens, place, after=()):
        pick = tables(lax.dynamic_slice_in_dim(tokens, place, META, 1), tok, top, wanted, capacity)
        rows = dispatch(*pick, tokens, cols, capacity, after)
        return rows, lax.all_to_all(rows, ("y", "c"), 0, 0, tiled=True)

    rows0, arrived0 = exchange(gathered[0], cols, (traded,))
    flag = later(flag_here, rows0)
    own = jnp.where(flag == 1, traded, hidden).transpose(0, 2, 1, 3, 4)
    own = own.reshape(NY * NC, NZ * capacity, width)
    left = lax.ppermute(own, "x", ring(NX, 1))
    right = lax.ppermute(own, "x", ring(NX, 3))
    rows1, arrived1 = exchange(gathered[1], later(cols, own))
    half = own.shape[0] // 2
    start = later(0, rows1)
    far = [
        lax.ppermute(lax.dynamic_slice_in_dim(left, start, half), "x", ring(NX, 1)),
        lax.ppermute(lax.dynamic_slice_in_dim(right, start + half, half), "x", ring(NX, 3)),
    ]
    total = product(None, arrived0, [[own], [left]])
    total = product(total, arrived1, [[right], far])
    return total[None]


def solution(mesh):
    fine = Mesh(mesh.devices.reshape(NX, NY, NZ, NC), ("x", "y", "z", "c"))
    every = ("x", "y", "z", "c")
    return jax.shard_map(
        local,
        mesh=fine,
        in_specs=(
            P(every, None),
            P(every, None),
            P(every, None),
            P("x", ("y", "z", "c"), None, None, None),
            P(),
        ),
        out_specs=P(("y", "z", "c"), "x", None),
        check_vma=False,
    )
```

```python
import functools

import jax
import jax.numpy as jnp
from jax import lax
from jax.experimental import pallas as pl
from jax.experimental.pallas import tpu as pltpu
from jax.sharding import Mesh, PartitionSpec as P

NX, NY, NZ, NC = 4, 4, 8, 2
GATHERS = ((0,), (1, 3), (2,))
SPACE = 56 * 1024 * 1024
PARTS = 3
META = 128
LIGHT = pl.CostEstimate(flops=1024, bytes_accessed=1024, transcendentals=0)


def dispatch_kernel(target_ref, gate_ref, token_ref, *refs):
    out_ref = refs[-1]
    dests, rows = out_ref.shape[:2]
    tokens = target_ref.shape[2]
    slot = lax.broadcasted_iota(jnp.int32, (rows, tokens), 0).astype(jnp.float32)
    picks, weights = [], []
    for r in range(dests):
        hit = slot == target_ref[0, r : r + 1, :]
        picks.append(jnp.where(hit, 1.0, 0.0))
        weights.append(jnp.sum(jnp.where(hit, gate_ref[0, r : r + 1, :], 0.0), axis=1, keepdims=True))
    pick = jnp.concatenate(picks, axis=0).astype(jnp.bfloat16)
    weight = jnp.concatenate(weights, axis=0)
    scaled = jnp.dot(pick, token_ref[...], preferred_element_type=jnp.float32) * weight
    scaled = scaled.astype(jnp.bfloat16)
    for r in range(dests):
        out_ref[r] = scaled[r * rows : (r + 1) * rows]


def dispatch(target, gate, tokens, cols, capacity, after=()):
    pairs, dests, width = target.shape
    rows = 2 * capacity
    return pl.pallas_call(
        dispatch_kernel,
        grid=(pairs,),
        in_specs=[
            pl.BlockSpec((1, dests, width), lambda i: (i, 0, 0)),
            pl.BlockSpec((1, dests, width), lambda i: (i, 0, 0)),
            pl.BlockSpec((width, cols), lambda i: (i, 0)),
        ]
        + [pl.BlockSpec(memory_space=pl.ANY)] * len(after),
        out_specs=pl.BlockSpec((dests, rows, cols), lambda i: (0, i, 0)),
        out_shape=jax.ShapeDtypeStruct((dests, pairs * rows, cols), jnp.bfloat16),
        compiler_params=pltpu.CompilerParams(vmem_limit_bytes=SPACE),
        cost_estimate=LIGHT,
    )(target, gate, tokens, *after)


def later_kernel(value_ref, *refs):
    refs[-1][0] = value_ref[0]


def later(value, *after):
    return pl.pallas_call(
        later_kernel,
        in_specs=[pl.BlockSpec(memory_space=pltpu.SMEM)] + [pl.BlockSpec(memory_space=pl.ANY)] * len(after),
        out_specs=pl.BlockSpec(memory_space=pltpu.SMEM),
        out_shape=jax.ShapeDtypeStruct((1,), jnp.int32),
        cost_estimate=LIGHT,
    )(jnp.asarray(value, jnp.int32).reshape(1), *after)[0]


def ring(size, step):
    return [(i, (i + step) % size) for i in range(size)]


def routing(ids, gates):
    columns = [ids.astype(jnp.float32)]
    for _ in range(PARTS):
        high = lax.reduce_precision(gates, 8, 7)
        columns.append(high)
        gates = gates - high
    meta = jnp.concatenate(columns, axis=1)
    return jnp.pad(meta, ((0, 0), (0, META - meta.shape[1]))).astype(jnp.bfloat16)


def tables(meta, tok, top, wanted, capacity):
    sources = meta.shape[0] // tok
    meta = meta.astype(jnp.float32).reshape(sources, tok, -1).transpose(0, 2, 1)
    ids, gates = meta[:, :top], 0.0
    for i in reversed(range(PARTS)):
        gates = gates + meta[:, (i + 1) * top : (i + 2) * top]
    match = ids[:, None] == wanted[None, :, None, None]
    member = jnp.any(match, axis=2)
    gate = jnp.sum(jnp.where(match, gates[:, None], 0.0), axis=2)
    before = (jnp.arange(tok)[:, None] < jnp.arange(tok)[None, :]).astype(jnp.bfloat16)
    slot = jnp.dot(member.astype(jnp.bfloat16), before, preferred_element_type=jnp.float32)
    odd = (jnp.arange(sources) % 2 * capacity).astype(jnp.float32)
    target = jnp.where(member, slot + odd[:, None, None], -1.0)

    def paired(table):
        table = table.reshape(sources // 2, 2, len(wanted), tok).transpose(0, 2, 1, 3)
        return table.reshape(sources // 2, len(wanted), 2 * tok)

    return paired(target), paired(gate)


def product_kernel(spans, *refs):
    rows_ref, states, out_ref = refs[0], refs[1 : 1 + len(spans)], refs[-1]
    step = pl.program_id(0)

    @pl.when(step == 0)
    def _():
        out_ref[...] = refs[-2][...] if len(refs) > len(spans) + 2 else jnp.zeros_like(out_ref)

    depth, width = states[0].shape[1:]

    def add(chunk, states_ref):
        rows = rows_ref[:, chunk * depth : (chunk + 1) * depth, :]
        out_ref[...] += lax.dot_general(
            rows.reshape(-1, rows.shape[-1]),
            states_ref[...].reshape(-1, width),
            (((0,), (0,)), ((), ())),
            preferred_element_type=jnp.float32,
        )

    for (chunk, low, high), states_ref in zip(spans, states):
        pl.when((step >= low) & (step < high))(functools.partial(add, chunk, states_ref))


def product(total, rows, states):
    senders, _, cols = rows.shape
    group = senders // 2
    depth, width = states[0][0].shape[1:]
    whole = pl.BlockSpec((cols, width), lambda i: (0, 0))
    spans, arrays, specs = [], [], []
    for chunk, parts in enumerate(states):
        low = 0
        for array in parts:
            count = array.shape[0] // group
            spans.append((chunk, low, low + count))
            arrays.append(array)
            specs.append(
                pl.BlockSpec(
                    (group, depth, width),
                    functools.partial(lambda low, count, i: (jnp.clip(i - low, 0, count - 1), 0, 0), low, count),
                )
            )
            low += count
    return pl.pallas_call(
        functools.partial(product_kernel, tuple(spans)),
        grid=(senders // group,),
        in_specs=[pl.BlockSpec((group,) + rows.shape[1:], lambda i: (i, 0, 0))]
        + specs
        + ([] if total is None else [whole]),
        out_specs=whole,
        out_shape=jax.ShapeDtypeStruct((cols, width), jnp.float32),
        compiler_params=pltpu.CompilerParams(vmem_limit_bytes=SPACE),
        cost_estimate=LIGHT,
    )(rows, *arrays, *([] if total is None else [total]))


def local(grad_out, expert_ids, gate_weights, hidden_saved, swap_flags):
    x, y = lax.axis_index("x"), lax.axis_index("y")
    z, c = lax.axis_index("z"), lax.axis_index("c")
    experts, capacity, width = hidden_saved.shape[2:]
    tok, cols = grad_out.shape[0], grad_out.shape[1] // NX
    top = expert_ids.shape[1]
    flag_here = lax.dynamic_index_in_dim(swap_flags, (y * NZ + z) * NC + c, 0, False)
    hidden = hidden_saved.reshape(NY, NZ, NC, capacity, width)
    traded = lax.ppermute(hidden, "y", ring(NY, 2))

    meta = routing(expert_ids, gate_weights)

    def columns(step):
        part = lax.dynamic_slice_in_dim(grad_out, ((x + step) % NX) * cols, cols, 1)
        part = jnp.concatenate([part, meta], axis=1)
        return part if step == 0 else lax.ppermute(part, "x", ring(NX, step))

    gathered = []
    for group in GATHERS:
        block = jnp.stack([columns(s) for s in group])
        gathered.append(lax.all_gather(block, "z", axis=1, tiled=True).reshape(-1, cols + META))

    devices = ((jnp.arange(NY)[:, None] * NZ + z) * NC + jnp.arange(NC)[None]).reshape(-1)
    flags = jnp.take(swap_flags, devices)
    wanted = jnp.where(flags == 1, (devices + experts // 2) % experts, devices).astype(jnp.float32)

    def exchange(tokens, place, after=()):
        pick = tables(lax.dynamic_slice_in_dim(tokens, place, META, 1), tok, top, wanted, capacity)
        rows = dispatch(*pick, tokens, cols, capacity, after)
        return rows, lax.all_to_all(rows, ("y", "c"), 0, 0, tiled=True)

    rows0, arrived0 = exchange(gathered[0], cols)
    flag = later(flag_here, rows0)
    own = jnp.where(flag == 1, traded, hidden).transpose(0, 2, 1, 3, 4)
    own = own.reshape(NY * NC, NZ * capacity, width)
    left = lax.ppermute(own, "x", ring(NX, 1))
    right = lax.ppermute(own, "x", ring(NX, 3))
    rows1, arrived1 = exchange(gathered[1], later(cols, own))
    half = own.shape[0] // 2
    start = later(0, rows1)
    far = [
        lax.ppermute(lax.dynamic_slice_in_dim(left, start, half), "x", ring(NX, 1)),
        lax.ppermute(lax.dynamic_slice_in_dim(right, start + half, half), "x", ring(NX, 3)),
    ]
    total = product(None, arrived0, [[own]])
    rows2, arrived2 = exchange(gathered[2], later(cols, rows1, total))
    total = product(total, arrived1, [[left], [right]])
    total = product(total, arrived2, [far])
    return total[None]


def solution(mesh):
    fine = Mesh(mesh.devices.reshape(NX, NY, NZ, NC), ("x", "y", "z", "c"))
    every = ("x", "y", "z", "c")
    return jax.shard_map(
        local,
        mesh=fine,
        in_specs=(
            P(every, None),
            P(every, None),
            P(every, None),
            P("x", ("y", "z", "c"), None, None, None),
            P(),
        ),
        out_specs=P(("y", "z", "c"), "x", None),
        check_vma=False,
    )
```

```python
import functools

import jax
import jax.numpy as jnp
from jax import lax
from jax.experimental import pallas as pl
from jax.experimental.pallas import tpu as pltpu
from jax.sharding import Mesh, PartitionSpec as P

NX, NY, NZ, NC = 4, 4, 8, 2
GATHERS = ((0,), (1, 3), (2,))
SPACE = 56 * 1024 * 1024
PARTS = 3
META = 128
HEAVY = pl.CostEstimate(flops=2 * 10**11, bytes_accessed=10**8, transcendentals=0)
LIGHT = pl.CostEstimate(flops=1024, bytes_accessed=1024, transcendentals=0)


def dispatch_kernel(target_ref, gate_ref, token_ref, *refs):
    out_ref = refs[-1]
    dests, rows = out_ref.shape[:2]
    tokens = target_ref.shape[2]
    slot = lax.broadcasted_iota(jnp.int32, (rows, tokens), 0).astype(jnp.float32)
    picks, weights = [], []
    for r in range(dests):
        hit = slot == target_ref[0, r : r + 1, :]
        picks.append(jnp.where(hit, 1.0, 0.0))
        weights.append(jnp.sum(jnp.where(hit, gate_ref[0, r : r + 1, :], 0.0), axis=1, keepdims=True))
    pick = jnp.concatenate(picks, axis=0).astype(jnp.bfloat16)
    weight = jnp.concatenate(weights, axis=0)
    scaled = jnp.dot(pick, token_ref[...], preferred_element_type=jnp.float32) * weight
    scaled = scaled.astype(jnp.bfloat16)
    for r in range(dests):
        out_ref[r] = scaled[r * rows : (r + 1) * rows]


def dispatch(target, gate, tokens, cols, capacity, after=()):
    pairs, dests, width = target.shape
    rows = 2 * capacity
    return pl.pallas_call(
        dispatch_kernel,
        grid=(pairs,),
        in_specs=[
            pl.BlockSpec((1, dests, width), lambda i: (i, 0, 0)),
            pl.BlockSpec((1, dests, width), lambda i: (i, 0, 0)),
            pl.BlockSpec((width, cols), lambda i: (i, 0)),
        ]
        + [pl.BlockSpec(memory_space=pl.ANY)] * len(after),
        out_specs=pl.BlockSpec((dests, rows, cols), lambda i: (0, i, 0)),
        out_shape=jax.ShapeDtypeStruct((dests, pairs * rows, cols), jnp.bfloat16),
        compiler_params=pltpu.CompilerParams(vmem_limit_bytes=SPACE),
        cost_estimate=LIGHT,
    )(target, gate, tokens, *after)


def later_kernel(value_ref, *refs):
    refs[-1][0] = value_ref[0]


def later(value, *after):
    return pl.pallas_call(
        later_kernel,
        in_specs=[pl.BlockSpec(memory_space=pltpu.SMEM)] + [pl.BlockSpec(memory_space=pl.ANY)] * len(after),
        out_specs=pl.BlockSpec(memory_space=pltpu.SMEM),
        out_shape=jax.ShapeDtypeStruct((1,), jnp.int32),
        cost_estimate=LIGHT,
    )(jnp.asarray(value, jnp.int32).reshape(1), *after)[0]


def tied(value, *after):
    place = pl.BlockSpec(memory_space=pl.ANY)
    return pl.pallas_call(
        lambda *refs: None,
        in_specs=[place] * (1 + len(after)),
        out_specs=place,
        out_shape=jax.ShapeDtypeStruct(value.shape, value.dtype),
        input_output_aliases={0: 0},
        cost_estimate=LIGHT,
    )(value, *after)


def ring(size, step):
    return [(i, (i + step) % size) for i in range(size)]


def routing(ids, gates):
    columns = [ids.astype(jnp.float32)]
    for _ in range(PARTS):
        high = lax.reduce_precision(gates, 8, 7)
        columns.append(high)
        gates = gates - high
    meta = jnp.concatenate(columns, axis=1)
    return jnp.pad(meta, ((0, 0), (0, META - meta.shape[1]))).astype(jnp.bfloat16)


def tables(meta, tok, top, wanted, capacity):
    sources = meta.shape[0] // tok
    meta = meta.astype(jnp.float32).reshape(sources, tok, -1).transpose(0, 2, 1)
    ids, gates = meta[:, :top], 0.0
    for i in reversed(range(PARTS)):
        gates = gates + meta[:, (i + 1) * top : (i + 2) * top]
    match = ids[:, None] == wanted[None, :, None, None]
    member = jnp.any(match, axis=2)
    gate = jnp.sum(jnp.where(match, gates[:, None], 0.0), axis=2)
    before = (jnp.arange(tok)[:, None] < jnp.arange(tok)[None, :]).astype(jnp.bfloat16)
    slot = jnp.dot(member.astype(jnp.bfloat16), before, preferred_element_type=jnp.float32)
    odd = (jnp.arange(sources) % 2 * capacity).astype(jnp.float32)
    target = jnp.where(member, slot + odd[:, None, None], -1.0)

    def paired(table):
        table = table.reshape(sources // 2, 2, len(wanted), tok).transpose(0, 2, 1, 3)
        return table.reshape(sources // 2, len(wanted), 2 * tok)

    return paired(target), paired(gate)


def product_kernel(spans, summed, *refs):
    rows_ref, states, out_ref = refs[0], refs[1 : 1 + len(spans)], refs[-1]
    step = pl.program_id(0)

    @pl.when(step == 0)
    def _():
        out_ref[...] = refs[1 + len(spans)][...] if summed else jnp.zeros_like(out_ref)

    depth, width = states[0].shape[1:]

    def add(chunk, states_ref):
        rows = rows_ref[:, chunk * depth : (chunk + 1) * depth, :]
        out_ref[...] += lax.dot_general(
            rows.reshape(-1, rows.shape[-1]),
            states_ref[...].reshape(-1, width),
            (((0,), (0,)), ((), ())),
            preferred_element_type=jnp.float32,
        )

    for (chunk, low, high), states_ref in zip(spans, states):
        pl.when((step >= low) & (step < high))(functools.partial(add, chunk, states_ref))


def product(total, rows, states, after=(), cost=None):
    senders, _, cols = rows.shape
    group = senders // 2
    depth, width = states[0][0].shape[1:]
    whole = pl.BlockSpec((cols, width), lambda i: (0, 0))
    spans, arrays, specs = [], [], []
    for chunk, parts in enumerate(states):
        low = 0
        for array in parts:
            count = array.shape[0] // group
            spans.append((chunk, low, low + count))
            arrays.append(array)
            specs.append(
                pl.BlockSpec(
                    (group, depth, width),
                    functools.partial(lambda low, count, i: (jnp.clip(i - low, 0, count - 1), 0, 0), low, count),
                )
            )
            low += count
    return pl.pallas_call(
        functools.partial(product_kernel, tuple(spans), total is not None),
        grid=(senders // group,),
        in_specs=[pl.BlockSpec((group,) + rows.shape[1:], lambda i: (i, 0, 0))]
        + specs
        + ([] if total is None else [whole])
        + [pl.BlockSpec(memory_space=pl.ANY)] * len(after),
        out_specs=whole,
        out_shape=jax.ShapeDtypeStruct((cols, width), jnp.float32),
        compiler_params=pltpu.CompilerParams(vmem_limit_bytes=SPACE),
        cost_estimate=cost or LIGHT,
    )(rows, *arrays, *([] if total is None else [total]), *after)


def local(grad_out, expert_ids, gate_weights, hidden_saved, swap_flags):
    x, y = lax.axis_index("x"), lax.axis_index("y")
    z, c = lax.axis_index("z"), lax.axis_index("c")
    experts, capacity, width = hidden_saved.shape[2:]
    tok, cols = grad_out.shape[0], grad_out.shape[1] // NX
    top = expert_ids.shape[1]
    flag_here = lax.dynamic_index_in_dim(swap_flags, (y * NZ + z) * NC + c, 0, False)
    hidden = hidden_saved.reshape(NY, NZ, NC, capacity, width)
    traded = lax.ppermute(hidden, "y", ring(NY, 2))

    meta = routing(expert_ids, gate_weights)

    def columns(step):
        part = lax.dynamic_slice_in_dim(grad_out, ((x + step) % NX) * cols, cols, 1)
        part = jnp.concatenate([part, meta], axis=1)
        return part if step == 0 else lax.ppermute(part, "x", ring(NX, step))

    def gather(group, after=()):
        block = jnp.stack([columns(s) for s in group])
        block = tied(block, *after) if after else block
        return lax.all_gather(block, "z", axis=1, tiled=True).reshape(-1, cols + META)

    gathered = [gather(group) for group in GATHERS[:2]]

    devices = ((jnp.arange(NY)[:, None] * NZ + z) * NC + jnp.arange(NC)[None]).reshape(-1)
    flags = jnp.take(swap_flags, devices)
    wanted = jnp.where(flags == 1, (devices + experts // 2) % experts, devices).astype(jnp.float32)

    def exchange(tokens, place, after=()):
        pick = tables(lax.dynamic_slice_in_dim(tokens, place, META, 1), tok, top, wanted, capacity)
        rows = dispatch(*pick, tokens, cols, capacity, after)
        return rows, lax.all_to_all(rows, ("y", "c"), 0, 0, tiled=True)

    rows0, arrived0 = exchange(gathered[0], cols)
    flag = later(flag_here, rows0)
    own = jnp.where(flag == 1, traded, hidden).transpose(0, 2, 1, 3, 4)
    own = own.reshape(NY * NC, NZ * capacity, width)
    half = own.shape[0] // 2
    own = [own[:half], own[half:]]
    left0, right1 = lax.ppermute(own[0], "x", ring(NX, 1)), lax.ppermute(own[1], "x", ring(NX, 3))
    left1, right0 = lax.ppermute(own[1], "x", ring(NX, 1)), lax.ppermute(own[0], "x", ring(NX, 3))
    gathered.append(gather(GATHERS[2], (left0, right1)))
    rows1, arrived1 = exchange(gathered[1], later(cols, *own))
    left0, right1 = tied(left0, left1, right0), tied(right1, left1, right0)
    far = [lax.ppermute(left0, "x", ring(NX, 1)), lax.ppermute(right1, "x", ring(NX, 3))]
    total = product(None, arrived0, [own])
    rows2, arrived2 = exchange(gathered[2], later(cols, rows1, total))
    total = product(total, arrived1, [[left0, left1], [right0, right1]], (), HEAVY)
    total = product(total, arrived2, [far])
    return total[None]


def solution(mesh):
    fine = Mesh(mesh.devices.reshape(NX, NY, NZ, NC), ("x", "y", "z", "c"))
    every = ("x", "y", "z", "c")
    return jax.shard_map(
        local,
        mesh=fine,
        in_specs=(
            P(every, None),
            P(every, None),
            P(every, None),
            P("x", ("y", "z", "c"), None, None, None),
            P(),
        ),
        out_specs=P(("y", "z", "c"), "x", None),
        check_vma=False,
    )
```

```python
import functools

import jax
import jax.numpy as jnp
from jax import lax
from jax.experimental import pallas as pl
from jax.experimental.pallas import tpu as pltpu
from jax.sharding import Mesh, PartitionSpec as P

NX, NY, NZ, NC = 4, 4, 8, 2
GATHERS = ((0,), (1, 3), (2,))

SPACE = 56 * 1024 * 1024
PARTS = 3
META = 128
HEAVY = pl.CostEstimate(flops=2 * 10**11, bytes_accessed=10**8, transcendentals=0)
LIGHT = pl.CostEstimate(flops=1024, bytes_accessed=1024, transcendentals=0)


def dispatch_kernel(target_ref, gate_ref, token_ref, *refs):
    out_ref = refs[-1]
    pairs, dests, tokens = target_ref.shape
    rows = out_ref.shape[1] // pairs
    slot = lax.broadcasted_iota(jnp.int32, (rows, tokens), 0).astype(jnp.float32)
    for pair in range(pairs):
        picks, weights = [], []
        for r in range(dests):
            hit = slot == target_ref[pair, r : r + 1, :]
            picks.append(jnp.where(hit, 1.0, 0.0))
            weights.append(jnp.sum(jnp.where(hit, gate_ref[pair, r : r + 1, :], 0.0), axis=1, keepdims=True))
        pick = jnp.concatenate(picks, axis=0).astype(jnp.bfloat16)
        weight = jnp.concatenate(weights, axis=0)
        block = token_ref[pair * tokens : (pair + 1) * tokens, :]
        scaled = jnp.dot(pick, block, preferred_element_type=jnp.float32) * weight
        scaled = scaled.astype(jnp.bfloat16)
        for r in range(dests):
            out_ref[r, pair * rows : (pair + 1) * rows, :] = scaled[r * rows : (r + 1) * rows]


def dispatch(target, gate, tokens, cols, capacity, after=()):
    pairs, dests, width = target.shape
    rows = 2 * capacity
    group = max(1, pairs // 2)
    return pl.pallas_call(
        dispatch_kernel,
        grid=(pairs // group,),
        in_specs=[
            pl.BlockSpec((group, dests, width), lambda i: (i, 0, 0)),
            pl.BlockSpec((group, dests, width), lambda i: (i, 0, 0)),
            pl.BlockSpec((group * width, cols), lambda i: (i, 0)),
        ]
        + [pl.BlockSpec(memory_space=pl.ANY)] * len(after),
        out_specs=pl.BlockSpec((dests, group * rows, cols), lambda i: (0, i, 0)),
        out_shape=jax.ShapeDtypeStruct((dests, pairs * rows, cols), jnp.bfloat16),
        compiler_params=pltpu.CompilerParams(vmem_limit_bytes=SPACE),
        cost_estimate=LIGHT,
    )(target, gate, tokens, *after)


def later_kernel(value_ref, *refs):
    refs[-1][0] = value_ref[0]


def later(value, *after):
    return pl.pallas_call(
        later_kernel,
        in_specs=[pl.BlockSpec(memory_space=pltpu.SMEM)] + [pl.BlockSpec(memory_space=pl.ANY)] * len(after),
        out_specs=pl.BlockSpec(memory_space=pltpu.SMEM),
        out_shape=jax.ShapeDtypeStruct((1,), jnp.int32),
        cost_estimate=LIGHT,
    )(jnp.asarray(value, jnp.int32).reshape(1), *after)[0]


def tied(value, *after):
    place = pl.BlockSpec(memory_space=pl.ANY)
    return pl.pallas_call(
        lambda *refs: None,
        in_specs=[place] * (1 + len(after)),
        out_specs=place,
        out_shape=jax.ShapeDtypeStruct(value.shape, value.dtype),
        input_output_aliases={0: 0},
        cost_estimate=LIGHT,
    )(value, *after)


def ring(size, step):
    return [(i, (i + step) % size) for i in range(size)]


def routing(ids, gates):
    columns = [ids.astype(jnp.float32)]
    for _ in range(PARTS):
        high = lax.reduce_precision(gates, 8, 7)
        columns.append(high)
        gates = gates - high
    meta = jnp.concatenate(columns, axis=1)
    return jnp.pad(meta, ((0, 0), (0, META - meta.shape[1]))).astype(jnp.bfloat16)


def tables(meta, tok, top, wanted, capacity):
    sources = meta.shape[0] // tok
    meta = meta.astype(jnp.float32).reshape(sources, tok, -1).transpose(0, 2, 1)
    ids, gates = meta[:, :top], 0.0
    for i in reversed(range(PARTS)):
        gates = gates + meta[:, (i + 1) * top : (i + 2) * top]
    match = ids[:, None] == wanted[None, :, None, None]
    member = jnp.any(match, axis=2)
    gate = jnp.sum(jnp.where(match, gates[:, None], 0.0), axis=2)
    before = (jnp.arange(tok)[:, None] < jnp.arange(tok)[None, :]).astype(jnp.bfloat16)
    slot = jnp.dot(member.astype(jnp.bfloat16), before, preferred_element_type=jnp.float32)
    odd = (jnp.arange(sources) % 2 * capacity).astype(jnp.float32)
    target = jnp.where(member, slot + odd[:, None, None], -1.0)

    def paired(table):
        table = table.reshape(sources // 2, 2, len(wanted), tok).transpose(0, 2, 1, 3)
        return table.reshape(sources // 2, len(wanted), 2 * tok)

    return paired(target), paired(gate)


def product_kernel(spans, summed, *refs):
    rows_ref, states, out_ref = refs[0], refs[1 : 1 + len(spans)], refs[-1]
    step = pl.program_id(0)

    @pl.when(step == 0)
    def _():
        out_ref[...] = refs[1 + len(spans)][...] if summed else jnp.zeros_like(out_ref)

    depth, width = states[0].shape[1:]

    def add(chunk, states_ref):
        rows = rows_ref[:, chunk * depth : (chunk + 1) * depth, :]
        out_ref[...] += lax.dot_general(
            rows.reshape(-1, rows.shape[-1]),
            states_ref[...].reshape(-1, width),
            (((0,), (0,)), ((), ())),
            preferred_element_type=jnp.float32,
        )

    for (chunk, low, high), states_ref in zip(spans, states):
        pl.when((step >= low) & (step < high))(functools.partial(add, chunk, states_ref))


def product(total, rows, states, after=(), cost=None):
    senders, _, cols = rows.shape
    group = senders // 2
    depth, width = states[0][0].shape[1:]
    whole = pl.BlockSpec((cols, width), lambda i: (0, 0))
    spans, arrays, specs = [], [], []
    for chunk, parts in enumerate(states):
        low = 0
        for array in parts:
            count = array.shape[0] // group
            spans.append((chunk, low, low + count))
            arrays.append(array)
            specs.append(
                pl.BlockSpec(
                    (group, depth, width),
                    functools.partial(lambda low, count, i: (jnp.clip(i - low, 0, count - 1), 0, 0), low, count),
                )
            )
            low += count
    return pl.pallas_call(
        functools.partial(product_kernel, tuple(spans), total is not None),
        grid=(senders // group,),
        in_specs=[pl.BlockSpec((group,) + rows.shape[1:], lambda i: (i, 0, 0))]
        + specs
        + ([] if total is None else [whole])
        + [pl.BlockSpec(memory_space=pl.ANY)] * len(after),
        out_specs=whole,
        out_shape=jax.ShapeDtypeStruct((cols, width), jnp.float32),
        compiler_params=pltpu.CompilerParams(vmem_limit_bytes=SPACE),
        cost_estimate=cost or LIGHT,
    )(rows, *arrays, *([] if total is None else [total]), *after)


def local(grad_out, expert_ids, gate_weights, hidden_saved, swap_flags):
    x, y = lax.axis_index("x"), lax.axis_index("y")
    z, c = lax.axis_index("z"), lax.axis_index("c")
    experts, capacity, width = hidden_saved.shape[2:]
    tok, cols = grad_out.shape[0], grad_out.shape[1] // NX
    top = expert_ids.shape[1]
    flag_here = lax.dynamic_index_in_dim(swap_flags, (y * NZ + z) * NC + c, 0, False)
    traded = lax.ppermute(hidden_saved.reshape(-1, width), "y", ring(NY, 2))
    traded = traded.reshape(NY, NZ, NC, capacity, width)
    hidden = hidden_saved.reshape(traded.shape)

    meta = routing(expert_ids, gate_weights)

    def columns(step):
        part = lax.dynamic_slice_in_dim(grad_out, ((x + step) % NX) * cols, cols, 1)
        part = jnp.concatenate([part, meta], axis=1)
        return part if step == 0 else lax.ppermute(part, "x", ring(NX, step))

    def gather(group, after=()):
        block = jnp.stack([columns(s) for s in group])
        block = tied(block, *after) if after else block
        return lax.all_gather(block, "z", axis=1, tiled=True).reshape(-1, cols + META)

    gathered = [gather(group) for group in GATHERS[:2]]

    devices = ((jnp.arange(NY)[:, None] * NZ + z) * NC + jnp.arange(NC)[None]).reshape(-1)
    flags = jnp.take(swap_flags, devices)
    wanted = jnp.where(flags == 1, (devices + experts // 2) % experts, devices).astype(jnp.float32)

    def exchange(tokens, place, after=()):
        pick = tables(lax.dynamic_slice_in_dim(tokens, place, META, 1), tok, top, wanted, capacity)
        rows = dispatch(*pick, tokens, cols, capacity, after)
        return rows, lax.all_to_all(rows, ("y", "c"), 0, 0, tiled=True)

    rows0, arrived0 = exchange(gathered[0], cols)
    flag = later(flag_here, rows0)
    own = jnp.where(flag == 1, traded, hidden).transpose(0, 2, 1, 3, 4)
    own = own.reshape(NY * NC, NZ * capacity, width)
    half = own.shape[0] // 2
    own = [own[:half], own[half:]]
    left0, right1 = lax.ppermute(own[0], "x", ring(NX, 1)), lax.ppermute(own[1], "x", ring(NX, 3))
    left1, right0 = lax.ppermute(own[1], "x", ring(NX, 1)), lax.ppermute(own[0], "x", ring(NX, 3))
    gathered.append(gather(GATHERS[2], (left0, right1)))
    rows1, arrived1 = exchange(gathered[1], later(cols, *own))
    left0, right1 = tied(left0, left1, right0), tied(right1, left1, right0)
    far = [lax.ppermute(left0, "x", ring(NX, 1)), lax.ppermute(right1, "x", ring(NX, 3))]
    total = product(None, arrived0, [own])
    rows2, arrived2 = exchange(gathered[2], later(cols, rows1, total))
    total = product(total, arrived1, [[left0, left1], [right0, right1]], (), HEAVY)
    total = product(total, arrived2, [far])
    return total[None]


def solution(mesh):
    fine = Mesh(mesh.devices.reshape(NX, NY, NZ, NC), ("x", "y", "z", "c"))
    every = ("x", "y", "z", "c")
    return jax.shard_map(
        local,
        mesh=fine,
        in_specs=(
            P(every, None),
            P(every, None),
            P(every, None),
            P("x", ("y", "z", "c"), None, None, None),
            P(),
        ),
        out_specs=P(("y", "z", "c"), "x", None),
        check_vma=False,
    )
```

```python
import functools

import jax
import jax.numpy as jnp
from jax import lax
from jax.experimental import pallas as pl
from jax.experimental.pallas import tpu as pltpu
from jax.sharding import Mesh, PartitionSpec as P

NX, NY, NZ, NC = 4, 4, 8, 2
GATHERS = ((0,), (1, 3), (2,))

SPACE = 56 * 1024 * 1024
PARTS = 3
META = 128
HEAVY = pl.CostEstimate(flops=2 * 10**11, bytes_accessed=10**8, transcendentals=0)
LIGHT = pl.CostEstimate(flops=1024, bytes_accessed=1024, transcendentals=0)


def dispatch_kernel(tok, top, capacity, cols, wanted_ref, token_ref, *refs):
    out_ref = refs[-1]
    dests, rows, width = wanted_ref.shape[0], 2 * capacity, 2 * tok
    slot = lax.broadcasted_iota(jnp.int32, (rows, width), 0).astype(jnp.float32)
    before = lax.broadcasted_iota(jnp.int32, (tok, tok), 0) < lax.broadcasted_iota(jnp.int32, (tok, tok), 1)
    before = jnp.where(before, 1.0, 0.0).astype(jnp.bfloat16)
    for pair in range(token_ref.shape[0] // width):
        span = slice(pair * width, (pair + 1) * width)
        meta = token_ref[span, cols:].astype(jnp.float32).T
        ids, gates = meta[:top], 0.0
        for i in reversed(range(PARTS)):
            gates = gates + meta[(i + 1) * top : (i + 2) * top]
        members, chosen = [], []
        for r in range(dests):
            match = ids == wanted_ref[r]
            members.append(jnp.sum(jnp.where(match, 1.0, 0.0), axis=0, keepdims=True))
            chosen.append(jnp.sum(jnp.where(match, gates, 0.0), axis=0, keepdims=True))
        member = jnp.concatenate(members, axis=0)
        member = jnp.concatenate([member[:, :tok], member[:, tok:]], axis=0)
        place = jnp.dot(member.astype(jnp.bfloat16), before, preferred_element_type=jnp.float32)
        first = jnp.where(member[:dests] > 0.5, place[:dests], -1.0)
        second = jnp.where(member[dests:] > 0.5, place[dests:] + capacity, -1.0)
        target = jnp.concatenate([first, second], axis=1)
        picks, weights = [], []
        for r in range(dests):
            hit = slot == target[r : r + 1, :]
            picks.append(jnp.where(hit, 1.0, 0.0))
            weights.append(jnp.sum(jnp.where(hit, chosen[r], 0.0), axis=1, keepdims=True))
        pick = jnp.concatenate(picks, axis=0).astype(jnp.bfloat16)
        weight = jnp.concatenate(weights, axis=0)
        scaled = jnp.dot(pick, token_ref[span, :cols], preferred_element_type=jnp.float32) * weight
        scaled = scaled.astype(jnp.bfloat16)
        for r in range(dests):
            out_ref[r, pair * rows : (pair + 1) * rows, :] = scaled[r * rows : (r + 1) * rows]


def dispatch(wanted, tokens, tok, top, capacity, after=()):
    total, dests = tokens.shape[0], wanted.shape[0]
    cols, rows = tokens.shape[1] - META, total // tok * capacity
    steps = 2
    return pl.pallas_call(
        functools.partial(dispatch_kernel, tok, top, capacity, cols),
        grid=(steps,),
        in_specs=[
            pl.BlockSpec(memory_space=pltpu.SMEM),
            pl.BlockSpec((total // steps, tokens.shape[1]), lambda i: (i, 0)),
        ]
        + [pl.BlockSpec(memory_space=pl.ANY)] * len(after),
        out_specs=pl.BlockSpec((dests, rows // steps, cols), lambda i: (0, i, 0)),
        out_shape=jax.ShapeDtypeStruct((dests, rows, cols), jnp.bfloat16),
        compiler_params=pltpu.CompilerParams(vmem_limit_bytes=SPACE),
        cost_estimate=LIGHT,
    )(wanted, tokens, *after)


def later_kernel(value_ref, *refs):
    refs[-1][0] = value_ref[0]


def later(value, *after):
    return pl.pallas_call(
        later_kernel,
        in_specs=[pl.BlockSpec(memory_space=pltpu.SMEM)] + [pl.BlockSpec(memory_space=pl.ANY)] * len(after),
        out_specs=pl.BlockSpec(memory_space=pltpu.SMEM),
        out_shape=jax.ShapeDtypeStruct((1,), jnp.int32),
        cost_estimate=LIGHT,
    )(jnp.asarray(value, jnp.int32).reshape(1), *after)[0]


def tied(value, *after):
    place = pl.BlockSpec(memory_space=pl.ANY)
    return pl.pallas_call(
        lambda *refs: None,
        in_specs=[place] * (1 + len(after)),
        out_specs=place,
        out_shape=jax.ShapeDtypeStruct(value.shape, value.dtype),
        input_output_aliases={0: 0},
        cost_estimate=LIGHT,
    )(value, *after)


def ring(size, step):
    return [(i, (i + step) % size) for i in range(size)]


def routing(ids, gates):
    columns = [ids.astype(jnp.float32)]
    for _ in range(PARTS):
        high = lax.reduce_precision(gates, 8, 7)
        columns.append(high)
        gates = gates - high
    meta = jnp.concatenate(columns, axis=1)
    return jnp.pad(meta, ((0, 0), (0, META - meta.shape[1]))).astype(jnp.bfloat16)


def product_kernel(spans, summed, *refs):
    rows_ref, states, out_ref = refs[0], refs[1 : 1 + len(spans)], refs[-1]
    step = pl.program_id(0)

    @pl.when(step == 0)
    def _():
        out_ref[...] = refs[1 + len(spans)][...] if summed else jnp.zeros_like(out_ref)

    depth, width = states[0].shape[1:]

    def add(chunk, states_ref):
        rows = rows_ref[:, chunk * depth : (chunk + 1) * depth, :]
        out_ref[...] += lax.dot_general(
            rows.reshape(-1, rows.shape[-1]),
            states_ref[...].reshape(-1, width),
            (((0,), (0,)), ((), ())),
            preferred_element_type=jnp.float32,
        )

    for (chunk, low, high), states_ref in zip(spans, states):
        pl.when((step >= low) & (step < high))(functools.partial(add, chunk, states_ref))


def product(total, rows, states, after=(), cost=None):
    senders, _, cols = rows.shape
    group = senders // 2
    depth, width = states[0][0].shape[1:]
    whole = pl.BlockSpec((cols, width), lambda i: (0, 0))
    spans, arrays, specs = [], [], []
    for chunk, parts in enumerate(states):
        low = 0
        for array in parts:
            count = array.shape[0] // group
            spans.append((chunk, low, low + count))
            arrays.append(array)
            specs.append(
                pl.BlockSpec(
                    (group, depth, width),
                    functools.partial(lambda low, count, i: (jnp.clip(i - low, 0, count - 1), 0, 0), low, count),
                )
            )
            low += count
    return pl.pallas_call(
        functools.partial(product_kernel, tuple(spans), total is not None),
        grid=(senders // group,),
        in_specs=[pl.BlockSpec((group,) + rows.shape[1:], lambda i: (i, 0, 0))]
        + specs
        + ([] if total is None else [whole])
        + [pl.BlockSpec(memory_space=pl.ANY)] * len(after),
        out_specs=whole,
        out_shape=jax.ShapeDtypeStruct((cols, width), jnp.float32),
        compiler_params=pltpu.CompilerParams(vmem_limit_bytes=SPACE),
        cost_estimate=cost or LIGHT,
    )(rows, *arrays, *([] if total is None else [total]), *after)


def local(grad_out, expert_ids, gate_weights, hidden_saved, swap_flags):
    x, y = lax.axis_index("x"), lax.axis_index("y")
    z, c = lax.axis_index("z"), lax.axis_index("c")
    experts, capacity, width = hidden_saved.shape[2:]
    tok, cols = grad_out.shape[0], grad_out.shape[1] // NX
    top = expert_ids.shape[1]
    flag_here = lax.dynamic_index_in_dim(swap_flags, (y * NZ + z) * NC + c, 0, False)
    traded = lax.ppermute(hidden_saved.reshape(-1, width), "y", ring(NY, 2))
    traded = traded.reshape(NY, NZ, NC, capacity, width)
    hidden = hidden_saved.reshape(traded.shape)

    meta = routing(expert_ids, gate_weights)

    def columns(step):
        part = lax.dynamic_slice_in_dim(grad_out, ((x + step) % NX) * cols, cols, 1)
        part = jnp.concatenate([part, meta], axis=1)
        return part if step == 0 else lax.ppermute(part, "x", ring(NX, step))

    def gather(group, after=()):
        block = jnp.stack([columns(s) for s in group])
        block = tied(block, *after) if after else block
        return lax.all_gather(block, "z", axis=1, tiled=True).reshape(-1, cols + META)

    gathered = [gather(group) for group in GATHERS[:2]]

    devices = ((jnp.arange(NY)[:, None] * NZ + z) * NC + jnp.arange(NC)[None]).reshape(-1)
    flags = jnp.take(swap_flags, devices)
    wanted = jnp.where(flags == 1, (devices + experts // 2) % experts, devices).astype(jnp.float32)

    def exchange(tokens, after=()):
        rows = dispatch(wanted, tokens, tok, top, capacity, after)
        return rows, lax.all_to_all(rows, ("y", "c"), 0, 0, tiled=True)

    rows0, arrived0 = exchange(gathered[0])
    flag = later(flag_here, rows0)
    own = jnp.where(flag == 1, traded, hidden).transpose(0, 2, 1, 3, 4)
    own = own.reshape(NY * NC, NZ * capacity, width)
    half = own.shape[0] // 2
    own = [own[:half], own[half:]]
    left0, right1 = lax.ppermute(own[0], "x", ring(NX, 1)), lax.ppermute(own[1], "x", ring(NX, 3))
    left1, right0 = lax.ppermute(own[1], "x", ring(NX, 1)), lax.ppermute(own[0], "x", ring(NX, 3))
    gathered.append(gather(GATHERS[2], (left0, right1)))
    rows1, arrived1 = exchange(gathered[1], tuple(own))
    left0, right1 = tied(left0, left1, right0), tied(right1, left1, right0)
    far = [lax.ppermute(left0, "x", ring(NX, 1)), lax.ppermute(right1, "x", ring(NX, 3))]
    total = product(None, arrived0, [own])
    rows2, arrived2 = exchange(gathered[2], (rows1, total))
    total = product(total, arrived1, [[left0, left1], [right0, right1]], (), HEAVY)
    total = product(total, arrived2, [far])
    return total[None]


def solution(mesh):
    fine = Mesh(mesh.devices.reshape(NX, NY, NZ, NC), ("x", "y", "z", "c"))
    every = ("x", "y", "z", "c")
    return jax.shard_map(
        local,
        mesh=fine,
        in_specs=(
            P(every, None),
            P(every, None),
            P(every, None),
            P("x", ("y", "z", "c"), None, None, None),
            P(),
        ),
        out_specs=P(("y", "z", "c"), "x", None),
        check_vma=False,
    )
```

```python
import functools

import jax
import jax.numpy as jnp
from jax import lax
from jax.experimental import pallas as pl
from jax.experimental.pallas import tpu as pltpu
from jax.sharding import Mesh, PartitionSpec as P

NX, NY, NZ, NC = 4, 4, 8, 2
GATHERS = ((0,), (1, 3), (2,))

SPACE = 56 * 1024 * 1024
PARTS = 3
META = 128
HEAVY = pl.CostEstimate(flops=2 * 10**11, bytes_accessed=10**8, transcendentals=0)
LIGHT = pl.CostEstimate(flops=1024, bytes_accessed=1024, transcendentals=0)


def dispatch_kernel(tok, top, capacity, cols, wanted_ref, token_ref, *refs):
    out_ref = refs[-1]
    dests, rows, width = wanted_ref.shape[0], 2 * capacity, 2 * tok
    slot = lax.broadcasted_iota(jnp.int32, (rows, width), 0).astype(jnp.float32)
    before = lax.broadcasted_iota(jnp.int32, (tok, tok), 0) < lax.broadcasted_iota(jnp.int32, (tok, tok), 1)
    before = jnp.where(before, 1.0, 0.0).astype(jnp.bfloat16)
    for pair in range(token_ref.shape[0] // width):
        span = slice(pair * width, (pair + 1) * width)
        meta = token_ref[span, cols:].astype(jnp.float32).T
        ids, gates = meta[:top], 0.0
        for i in reversed(range(PARTS)):
            gates = gates + meta[(i + 1) * top : (i + 2) * top]
        members, chosen = [], []
        for r in range(dests):
            match = ids == wanted_ref[r]
            members.append(jnp.sum(jnp.where(match, 1.0, 0.0), axis=0, keepdims=True))
            chosen.append(jnp.sum(jnp.where(match, gates, 0.0), axis=0, keepdims=True))
        member = jnp.concatenate(members, axis=0)
        member = jnp.concatenate([member[:, :tok], member[:, tok:]], axis=0)
        place = jnp.dot(member.astype(jnp.bfloat16), before, preferred_element_type=jnp.float32)
        first = jnp.where(member[:dests] > 0.5, place[:dests], -1.0)
        second = jnp.where(member[dests:] > 0.5, place[dests:] + capacity, -1.0)
        target = jnp.concatenate([first, second], axis=1)
        picks, weights = [], []
        for r in range(dests):
            hit = slot == target[r : r + 1, :]
            picks.append(jnp.where(hit, 1.0, 0.0))
            weights.append(jnp.sum(jnp.where(hit, chosen[r], 0.0), axis=1, keepdims=True))
        pick = jnp.concatenate(picks, axis=0).astype(jnp.bfloat16)
        weight = jnp.concatenate(weights, axis=0)
        scaled = jnp.dot(pick, token_ref[span, :cols], preferred_element_type=jnp.float32) * weight
        scaled = scaled.astype(jnp.bfloat16)
        for r in range(dests):
            out_ref[r, pair * rows : (pair + 1) * rows, :] = scaled[r * rows : (r + 1) * rows]


def dispatch(wanted, tokens, tok, top, capacity, after=()):
    total, dests = tokens.shape[0], wanted.shape[0]
    cols, rows = tokens.shape[1] - META, total // tok * capacity
    steps = 2
    return pl.pallas_call(
        functools.partial(dispatch_kernel, tok, top, capacity, cols),
        grid=(steps,),
        in_specs=[
            pl.BlockSpec(memory_space=pltpu.SMEM),
            pl.BlockSpec((total // steps, tokens.shape[1]), lambda i: (i, 0)),
        ]
        + [pl.BlockSpec(memory_space=pl.ANY)] * len(after),
        out_specs=pl.BlockSpec((dests, rows // steps, cols), lambda i: (0, i, 0)),
        out_shape=jax.ShapeDtypeStruct((dests, rows, cols), jnp.bfloat16),
        compiler_params=pltpu.CompilerParams(vmem_limit_bytes=SPACE),
        cost_estimate=LIGHT,
    )(wanted, tokens, *after)


def later_kernel(value_ref, *refs):
    refs[-1][0] = value_ref[0]


def later(value, *after):
    return pl.pallas_call(
        later_kernel,
        in_specs=[pl.BlockSpec(memory_space=pltpu.SMEM)] + [pl.BlockSpec(memory_space=pl.ANY)] * len(after),
        out_specs=pl.BlockSpec(memory_space=pltpu.SMEM),
        out_shape=jax.ShapeDtypeStruct((1,), jnp.int32),
        cost_estimate=LIGHT,
    )(jnp.asarray(value, jnp.int32).reshape(1), *after)[0]


def tied(value, *after):
    place = pl.BlockSpec(memory_space=pl.ANY)
    return pl.pallas_call(
        lambda *refs: None,
        in_specs=[place] * (1 + len(after)),
        out_specs=place,
        out_shape=jax.ShapeDtypeStruct(value.shape, value.dtype),
        input_output_aliases={0: 0},
        cost_estimate=LIGHT,
    )(value, *after)


def ring(size, step):
    return [(i, (i + step) % size) for i in range(size)]


def routing(ids, gates):
    columns = [ids.astype(jnp.float32)]
    for _ in range(PARTS):
        high = lax.reduce_precision(gates, 8, 7)
        columns.append(high)
        gates = gates - high
    meta = jnp.concatenate(columns, axis=1)
    return jnp.pad(meta, ((0, 0), (0, META - meta.shape[1]))).astype(jnp.bfloat16)


def product_kernel(spans, summed, *refs):
    rows_ref, states, out_ref = refs[0], refs[1 : 1 + len(spans)], refs[-1]
    step = pl.program_id(0)

    @pl.when(step == 0)
    def _():
        out_ref[...] = refs[1 + len(spans)][...] if summed else jnp.zeros_like(out_ref)

    depth, width = states[0].shape[1:]

    def add(chunk, states_ref):
        rows = rows_ref[:, chunk * depth : (chunk + 1) * depth, :]
        out_ref[...] += lax.dot_general(
            rows.reshape(-1, rows.shape[-1]),
            states_ref[...].reshape(-1, width),
            (((0,), (0,)), ((), ())),
            preferred_element_type=jnp.float32,
        )

    for (chunk, low, high), states_ref in zip(spans, states):
        pl.when((step >= low) & (step < high))(functools.partial(add, chunk, states_ref))


def product(total, rows, states, after=(), cost=None):
    senders, _, cols = rows.shape
    group = senders // 2
    depth, width = states[0][0].shape[1:]
    whole = pl.BlockSpec((cols, width), lambda i: (0, 0))
    spans, arrays, specs = [], [], []
    for chunk, parts in enumerate(states):
        low = 0
        for array in parts:
            count = array.shape[0] // group
            spans.append((chunk, low, low + count))
            arrays.append(array)
            specs.append(
                pl.BlockSpec(
                    (group, depth, width),
                    functools.partial(lambda low, count, i: (jnp.clip(i - low, 0, count - 1), 0, 0), low, count),
                )
            )
            low += count
    return pl.pallas_call(
        functools.partial(product_kernel, tuple(spans), total is not None),
        grid=(senders // group,),
        in_specs=[pl.BlockSpec((group,) + rows.shape[1:], lambda i: (i, 0, 0))]
        + specs
        + ([] if total is None else [whole])
        + [pl.BlockSpec(memory_space=pl.ANY)] * len(after),
        out_specs=whole,
        out_shape=jax.ShapeDtypeStruct((cols, width), jnp.float32),
        compiler_params=pltpu.CompilerParams(vmem_limit_bytes=SPACE),
        cost_estimate=cost or LIGHT,
    )(rows, *arrays, *([] if total is None else [total]), *after)


def local(grad_out, expert_ids, gate_weights, hidden_saved, swap_flags):
    x, y = lax.axis_index("x"), lax.axis_index("y")
    z, c = lax.axis_index("z"), lax.axis_index("c")
    experts, capacity, width = hidden_saved.shape[2:]
    tok, cols = grad_out.shape[0], grad_out.shape[1] // NX
    top = expert_ids.shape[1]
    flag_here = lax.dynamic_index_in_dim(swap_flags, (y * NZ + z) * NC + c, 0, False)
    traded = lax.ppermute(hidden_saved.reshape(-1, width), "y", ring(NY, 2))
    traded = traded.reshape(NY, NZ, NC, capacity, width)
    hidden = hidden_saved.reshape(traded.shape)

    meta = routing(expert_ids, gate_weights)

    def columns(step):
        part = lax.dynamic_slice_in_dim(grad_out, ((x + step) % NX) * cols, cols, 1)
        part = jnp.concatenate([part, meta], axis=1)
        return part if step == 0 else lax.ppermute(part, "x", ring(NX, step))

    def gather(group, after=()):
        block = jnp.stack([columns(s) for s in group])
        block = tied(block, *after) if after else block
        return lax.all_gather(block, "z", axis=1, tiled=True).reshape(-1, cols + META)

    gathered = [gather(group) for group in GATHERS[:2]]

    devices = ((jnp.arange(NY)[:, None] * NZ + z) * NC + jnp.arange(NC)[None]).reshape(-1)
    flags = jnp.take(swap_flags, devices)
    wanted = jnp.where(flags == 1, (devices + experts // 2) % experts, devices).astype(jnp.float32)

    def exchange(tokens, after=()):
        rows = dispatch(wanted, tokens, tok, top, capacity, after)
        return rows, lax.all_to_all(rows, ("y", "c"), 0, 0, tiled=True)

    rows0, arrived0 = exchange(gathered[0])
    flag = later(flag_here, rows0)
    own = jnp.where(flag == 1, traded, hidden).transpose(0, 2, 1, 3, 4)
    own = own.reshape(NY * NC, NZ * capacity, width)
    half = own.shape[0] // 2
    own = [own[:half], own[half:]]
    left0, right1 = lax.ppermute(own[0], "x", ring(NX, 1)), lax.ppermute(own[1], "x", ring(NX, 3))
    left1, right0 = lax.ppermute(own[1], "x", ring(NX, 1)), lax.ppermute(own[0], "x", ring(NX, 3))
    total = product(None, arrived0, [own])
    gathered.append(gather(GATHERS[2], (left0, right1, total)))
    rows1, arrived1 = exchange(gathered[1], tuple(own))
    left0, right1 = tied(left0, left1, right0), tied(right1, left1, right0)
    far = [lax.ppermute(left0, "x", ring(NX, 1)), lax.ppermute(right1, "x", ring(NX, 3))]
    rows2, arrived2 = exchange(gathered[2], (rows1,))
    total = product(total, arrived1, [[left0, left1], [right0, right1]], (), HEAVY)
    total = product(total, arrived2, [far])
    return total[None]


def solution(mesh):
    fine = Mesh(mesh.devices.reshape(NX, NY, NZ, NC), ("x", "y", "z", "c"))
    every = ("x", "y", "z", "c")
    return jax.shard_map(
        local,
        mesh=fine,
        in_specs=(
            P(every, None),
            P(every, None),
            P(every, None),
            P("x", ("y", "z", "c"), None, None, None),
            P(),
        ),
        out_specs=P(("y", "z", "c"), "x", None),
        check_vma=False,
    )
```

```python
import functools

import jax
import jax.numpy as jnp
from jax import lax
from jax.experimental import pallas as pl
from jax.experimental.pallas import tpu as pltpu
from jax.sharding import Mesh, PartitionSpec as P

NX, NY, NZ, NC = 4, 4, 8, 2
GATHERS = ((0,), (1, 3), (2,))

SPACE = 56 * 1024 * 1024
PARTS = 3
META = 128
HEAVY = pl.CostEstimate(flops=2 * 10**11, bytes_accessed=10**8, transcendentals=0)
LIGHT = pl.CostEstimate(flops=1024, bytes_accessed=1024, transcendentals=0)


def dispatch_kernel(tok, top, capacity, cols, wanted_ref, token_ref, *refs):
    out_ref = refs[-1]
    dests, rows, width = wanted_ref.shape[0], 2 * capacity, 2 * tok
    slot = lax.broadcasted_iota(jnp.int32, (rows, width), 0).astype(jnp.float32)
    before = lax.broadcasted_iota(jnp.int32, (tok, tok), 0) < lax.broadcasted_iota(jnp.int32, (tok, tok), 1)
    before = jnp.where(before, 1.0, 0.0).astype(jnp.bfloat16)
    for pair in range(token_ref.shape[0] // width):
        span = slice(pair * width, (pair + 1) * width)
        meta = token_ref[span, cols:].astype(jnp.float32).T
        ids, gates = meta[:top], 0.0
        for i in reversed(range(PARTS)):
            gates = gates + meta[(i + 1) * top : (i + 2) * top]
        members, chosen = [], []
        for r in range(dests):
            match = ids == wanted_ref[r]
            members.append(jnp.sum(jnp.where(match, 1.0, 0.0), axis=0, keepdims=True))
            chosen.append(jnp.sum(jnp.where(match, gates, 0.0), axis=0, keepdims=True))
        member = jnp.concatenate(members, axis=0)
        member = jnp.concatenate([member[:, :tok], member[:, tok:]], axis=0)
        place = jnp.dot(member.astype(jnp.bfloat16), before, preferred_element_type=jnp.float32)
        first = jnp.where(member[:dests] > 0.5, place[:dests], -1.0)
        second = jnp.where(member[dests:] > 0.5, place[dests:] + capacity, -1.0)
        target = jnp.concatenate([first, second], axis=1)
        picks, weights = [], []
        for r in range(dests):
            hit = slot == target[r : r + 1, :]
            picks.append(jnp.where(hit, 1.0, 0.0))
            weights.append(jnp.sum(jnp.where(hit, chosen[r], 0.0), axis=1, keepdims=True))
        pick = jnp.concatenate(picks, axis=0).astype(jnp.bfloat16)
        weight = jnp.concatenate(weights, axis=0)
        scaled = jnp.dot(pick, token_ref[span, :cols], preferred_element_type=jnp.float32) * weight
        scaled = scaled.astype(jnp.bfloat16)
        for r in range(dests):
            out_ref[r, pair * rows : (pair + 1) * rows, :] = scaled[r * rows : (r + 1) * rows]


def dispatch(wanted, tokens, tok, top, capacity, after=()):
    total, dests = tokens.shape[0], wanted.shape[0]
    cols, rows = tokens.shape[1] - META, total // tok * capacity
    steps = 2
    return pl.pallas_call(
        functools.partial(dispatch_kernel, tok, top, capacity, cols),
        grid=(steps,),
        in_specs=[
            pl.BlockSpec(memory_space=pltpu.SMEM),
            pl.BlockSpec((total // steps, tokens.shape[1]), lambda i: (i, 0)),
        ]
        + [pl.BlockSpec(memory_space=pl.ANY)] * len(after),
        out_specs=pl.BlockSpec((dests, rows // steps, cols), lambda i: (0, i, 0)),
        out_shape=jax.ShapeDtypeStruct((dests, rows, cols), jnp.bfloat16),
        compiler_params=pltpu.CompilerParams(vmem_limit_bytes=SPACE),
        cost_estimate=LIGHT,
    )(wanted, tokens, *after)


def later_kernel(value_ref, *refs):
    refs[-1][0] = value_ref[0]


def later(value, *after):
    return pl.pallas_call(
        later_kernel,
        in_specs=[pl.BlockSpec(memory_space=pltpu.SMEM)] + [pl.BlockSpec(memory_space=pl.ANY)] * len(after),
        out_specs=pl.BlockSpec(memory_space=pltpu.SMEM),
        out_shape=jax.ShapeDtypeStruct((1,), jnp.int32),
        cost_estimate=LIGHT,
    )(jnp.asarray(value, jnp.int32).reshape(1), *after)[0]


def tied(value, *after):
    place = pl.BlockSpec(memory_space=pl.ANY)
    return pl.pallas_call(
        lambda *refs: None,
        in_specs=[place] * (1 + len(after)),
        out_specs=place,
        out_shape=jax.ShapeDtypeStruct(value.shape, value.dtype),
        input_output_aliases={0: 0},
        cost_estimate=LIGHT,
    )(value, *after)


def ring(size, step):
    return [(i, (i + step) % size) for i in range(size)]


def routing(ids, gates):
    columns = [ids.astype(jnp.float32)]
    for _ in range(PARTS):
        high = lax.reduce_precision(gates, 8, 7)
        columns.append(high)
        gates = gates - high
    meta = jnp.concatenate(columns, axis=1)
    return jnp.pad(meta, ((0, 0), (0, META - meta.shape[1]))).astype(jnp.bfloat16)


def product_kernel(spans, summed, *refs):
    rows_ref, states, out_ref = refs[0], refs[1 : 1 + len(spans)], refs[-1]
    step = pl.program_id(0)

    depth, width = states[0].shape[1:]

    def add(chunk, start, states_ref):
        rows = rows_ref[:, chunk * depth : (chunk + 1) * depth, :]
        term = lax.dot_general(
            rows.reshape(-1, rows.shape[-1]),
            states_ref[...].reshape(-1, width),
            (((0,), (0,)), ((), ())),
            preferred_element_type=jnp.float32,
        )
        if not start:
            out_ref[...] += term
        elif summed:
            out_ref[...] = refs[1 + len(spans)][...] + term
        else:
            out_ref[...] = term

    assert spans[0] == (0, 0, 1)
    for n, ((chunk, low, high), states_ref) in enumerate(zip(spans, states)):
        pl.when((step >= low) & (step < high))(functools.partial(add, chunk, n == 0, states_ref))


def product(total, rows, states, after=(), cost=None):
    senders, _, cols = rows.shape
    group = senders // 2
    depth, width = states[0][0].shape[1:]
    whole = pl.BlockSpec((cols, width), lambda i: (0, 0))
    spans, arrays, specs = [], [], []
    for chunk, parts in enumerate(states):
        low = 0
        for array in parts:
            count = array.shape[0] // group
            spans.append((chunk, low, low + count))
            arrays.append(array)
            specs.append(
                pl.BlockSpec(
                    (group, depth, width),
                    functools.partial(lambda low, count, i: (jnp.clip(i - low, 0, count - 1), 0, 0), low, count),
                )
            )
            low += count
    return pl.pallas_call(
        functools.partial(product_kernel, tuple(spans), total is not None),
        grid=(senders // group,),
        in_specs=[pl.BlockSpec((group,) + rows.shape[1:], lambda i: (i, 0, 0))]
        + specs
        + ([] if total is None else [whole])
        + [pl.BlockSpec(memory_space=pl.ANY)] * len(after),
        out_specs=whole,
        out_shape=jax.ShapeDtypeStruct((cols, width), jnp.float32),
        compiler_params=pltpu.CompilerParams(vmem_limit_bytes=SPACE),
        cost_estimate=cost or LIGHT,
    )(rows, *arrays, *([] if total is None else [total]), *after)


def local(grad_out, expert_ids, gate_weights, hidden_saved, swap_flags):
    x, y = lax.axis_index("x"), lax.axis_index("y")
    z, c = lax.axis_index("z"), lax.axis_index("c")
    experts, capacity, width = hidden_saved.shape[2:]
    tok, cols = grad_out.shape[0], grad_out.shape[1] // NX
    top = expert_ids.shape[1]
    flag_here = lax.dynamic_index_in_dim(swap_flags, (y * NZ + z) * NC + c, 0, False)
    traded = lax.ppermute(hidden_saved.reshape(-1, width), "y", ring(NY, 2))
    traded = traded.reshape(NY, NZ, NC, capacity, width)
    hidden = hidden_saved.reshape(traded.shape)

    meta = routing(expert_ids, gate_weights)

    def columns(step):
        part = lax.dynamic_slice_in_dim(grad_out, ((x + step) % NX) * cols, cols, 1)
        part = jnp.concatenate([part, meta], axis=1)
        return part if step == 0 else lax.ppermute(part, "x", ring(NX, step))

    def gather(group, after=()):
        block = jnp.stack([columns(s) for s in group])
        block = tied(block, *after) if after else block
        return lax.all_gather(block, "z", axis=1, tiled=True).reshape(-1, cols + META)

    gathered = [gather(group) for group in GATHERS[:2]]

    devices = ((jnp.arange(NY)[:, None] * NZ + z) * NC + jnp.arange(NC)[None]).reshape(-1)
    flags = jnp.take(swap_flags, devices)
    wanted = jnp.where(flags == 1, (devices + experts // 2) % experts, devices).astype(jnp.float32)

    def exchange(tokens, after=()):
        rows = dispatch(wanted, tokens, tok, top, capacity, after)
        return rows, lax.all_to_all(rows, ("y", "c"), 0, 0, tiled=True)

    rows0, arrived0 = exchange(gathered[0])
    flag = later(flag_here, rows0)
    own = jnp.where(flag == 1, traded, hidden).transpose(0, 2, 1, 3, 4)
    own = own.reshape(NY * NC, NZ * capacity, width)
    half = own.shape[0] // 2
    own = [own[:half], own[half:]]
    left0, right1 = lax.ppermute(own[0], "x", ring(NX, 1)), lax.ppermute(own[1], "x", ring(NX, 3))
    left1, right0 = lax.ppermute(own[1], "x", ring(NX, 1)), lax.ppermute(own[0], "x", ring(NX, 3))
    total = product(None, arrived0, [own])
    gathered.append(gather(GATHERS[2], (left0, right1, total)))
    rows1, arrived1 = exchange(gathered[1], tuple(own))
    left0, right1 = tied(left0, left1, right0), tied(right1, left1, right0)
    far = [lax.ppermute(left0, "x", ring(NX, 1)), lax.ppermute(right1, "x", ring(NX, 3))]
    rows2, arrived2 = exchange(gathered[2], (rows1,))
    total = product(total, arrived1, [[left0, left1], [right0, right1]], (), HEAVY)
    total = product(total, arrived2, [far])
    return total[None]


def solution(mesh):
    fine = Mesh(mesh.devices.reshape(NX, NY, NZ, NC), ("x", "y", "z", "c"))
    every = ("x", "y", "z", "c")
    return jax.shard_map(
        local,
        mesh=fine,
        in_specs=(
            P(every, None),
            P(every, None),
            P(every, None),
            P("x", ("y", "z", "c"), None, None, None),
            P(),
        ),
        out_specs=P(("y", "z", "c"), "x", None),
        check_vma=False,
    )
```
